256 devices in a mesh: blk: 16 (over z_lo, x, core), team: 16 (over y, z_hi).
Axes of the slice: x: 4, y: 4, z: 8 (z_hi: 4, z_lo: 2; z = z_hi * 2 + z_lo), core: 2. Of those that a mesh axis runs over, the one named last changes fastest.
Arguments:
- features: bfloat16 [32768, 256], P(('blk', 'team')), may hold values from -6 to 6
- weight: bfloat16 [256, 256], replicated, may hold values from -0.375 to 0.375
- grad_out: bfloat16 [32768, 256], P(('blk', 'team')), may hold values from -6 to 6
- block_vals: bfloat16 [256, 3, 16, 128, 128], P(('blk', 'team')), as said below
- block_rows: int32 [256, 3, 16], P(('blk', 'team')), may hold values from 0 to 255, as said below
- block_cols: int32 [256, 3, 16], P(('blk', 'team')), may hold values from 0 to 255, as said below
- block_counts: int32 [256, 3], P(('blk', 'team')), may hold values from 0 to 16, as said below
Outputs:
- activations: bfloat16 [32768, 256], P(('blk', 'team'))
- grad_feats: bfloat16 [32768, 256], P(('blk', 'team'))
- grad_weight: float32 [256, 256], replicated
The draws below stay inside these ranges and needn't reach their ends.
Inputs may be any that keep to these rules, and one draw needn't show every extreme that they name: `block_rows`: on the device at blk index b, every slot, used or not, names a block row of row slab b, that is b * 16 to (b + 1) * 16 - 1. `block_cols`: on the device at blk index b, every slot of offset s, used or not, names a block column of row slab (b + s - 1) mod 16. The first block_counts[d, s] slots of device d and offset s are used, the rest are to be ignored. Offset 1, the device's own slab, is full on every device. `block_vals`: no two used slots name the same block. A is symmetric: whenever block (R, C) is listed, block (C, R) is listed with the transposed values, and a block with R = C is symmetric itself.
All inputs are finite; a program needn't handle non-finite values.
Results may differ from the reference program's by a relative error of at most 0.0061.
Values may be sent and summed in bfloat16 or wider, within the bound.
No kernel may reach another device: no remote copies, remote signals or barrier semaphores. Data moves between devices by JAX's collectives and lax.ppermute only.
A program may use at most 64 MiB of HBM per device.

```python
import jax
import jax.numpy as jnp
from jax import lax

F_IN = 256
HID = 256
BS = 128
REACH = 1
SB = 16
CAP = 16
STEPS = 3
NODES = 32768
NBLOCKS = 256
N_BLK = 16
N_TEAM = 16
DEVICES = 256


def layout(key):
    block_total = SB * N_BLK
    hash_grid = jax.random.randint(jax.random.fold_in(key, 11), (block_total, block_total), 0, 8)
    row_pos = jnp.arange(block_total)[:, None]
    col_pos = jnp.arange(block_total)[None, :]
    hash_grid = jnp.where(row_pos <= col_pos, hash_grid, hash_grid.T)
    levels = jax.random.randint(jax.random.fold_in(key, 12), (N_BLK, N_BLK), 1, 9)
    slab_ids = jnp.arange(N_BLK)
    levels = jnp.where(slab_ids[:, None] <= slab_ids[None, :], levels, levels.T)
    device_ids = jnp.arange(DEVICES)[:, None, None]
    offset_ids = jnp.arange(STEPS)[None, :, None]
    slot_ids = jnp.arange(CAP)[None, None, :]
    full_shape = (DEVICES, STEPS, CAP)
    blk_of = device_ids // N_TEAM
    member = device_ids % N_TEAM
    position = member + N_TEAM * slot_ids
    local_row = position // SB
    local_col = (position % SB + local_row) % SB
    col_slab = (blk_of + offset_ids - REACH) % N_BLK
    row_ids = jnp.broadcast_to(blk_of * SB + local_row, full_shape)
    col_ids = jnp.broadcast_to(col_slab * SB + local_col, full_shape)
    in_use = jnp.where(col_slab == blk_of, True, hash_grid[row_ids, col_ids] < levels[blk_of, col_slab])
    in_use = jnp.broadcast_to(in_use, full_shape)
    sort_key = jnp.where(in_use, slot_ids, CAP + slot_ids)
    ordering = jnp.argsort(sort_key, axis=-1)
    row_ids = jnp.take_along_axis(row_ids, ordering, axis=-1).astype(jnp.int32)
    col_ids = jnp.take_along_axis(col_ids, ordering, axis=-1).astype(jnp.int32)
    used_slots = jnp.sum(in_use.astype(jnp.int32), axis=-1).astype(jnp.int32)
    return (row_ids, col_ids, used_slots)


def draw_block_rows(key, part):
    row_ids, col_ids, used_slots = layout(key)
    return row_ids


def draw_block_cols(key, part):
    row_ids, col_ids, used_slots = layout(key)
    return col_ids


def draw_block_counts(key, part):
    row_ids, col_ids, used_slots = layout(key)
    return used_slots


def draw_block_vals(key, part):
    row_ids, col_ids, used_slots = layout(key)
    key = jax.random.fold_in(key, 4)
    block_total = SB * N_BLK
    norm_scale = (2.0 * BS * SB) ** (-0.5)

    def one_block(lower_id, upper_id):
        return jax.random.normal(jax.random.fold_in(key, lower_id * block_total + upper_id), (BS, BS), jnp.float32)

    def one_device(device_idx):
        device_rows = row_ids[device_idx].reshape(-1)
        device_cols = col_ids[device_idx].reshape(-1)
        lower_id = jnp.minimum(device_rows, device_cols)
        upper_id = jnp.maximum(device_rows, device_cols)
        raw_tile = jax.vmap(one_block)(lower_id, upper_id)
        flipped = jnp.swapaxes(raw_tile, 1, 2)
        is_below = (device_rows > device_cols)[:, None, None]
        is_diag = (device_rows == device_cols)[:, None, None]
        tile_set = jnp.where(is_below, flipped, raw_tile)
        tile_set = jnp.where(is_diag, (raw_tile + flipped) * 0.7071067811865476, tile_set)
        return (tile_set * norm_scale).reshape(STEPS, CAP, BS, BS).astype(jnp.bfloat16)
    return lax.map(one_device, jnp.arange(DEVICES))


def shard_levels(key, shape, cuts, low, largest):
    def one(dim, blocks):
        draws = jax.random.uniform(jax.random.fold_in(jax.random.fold_in(key, 6), dim), (blocks,), jnp.float32, low / len(cuts), largest / len(cuts))
        return jnp.repeat(jnp.exp(draws), shape[dim] // blocks).reshape((-1,) + (1,) * (len(shape) - dim - 1))

    level = one(*cuts[0])
    for cut in cuts[1:]:
        level = level * one(*cut)
    return level


def centred(stream_key, shape, deviation, limit, cuts=(), kind=jnp.bfloat16):
    entries = deviation * jax.random.normal(stream_key, shape, jnp.float32)
    if cuts:
        entries = entries * shard_levels(stream_key, shape, cuts, -0.22, 0.18)
    return jnp.clip(entries, -limit, limit).astype(kind)


def setup_inputs(seed: int = 0) -> dict:
    streams_of = jax.random.split(jax.random.key(seed), 8)
    return {
        "features": centred(streams_of[0], (NODES, F_IN), 1.0, 6.0, ((0, 256),)),
        "weight": centred(streams_of[1], (F_IN, HID), F_IN ** -0.5, 0.375),
        "grad_out": centred(streams_of[2], (NODES, HID), 1.0, 6.0, ((0, 256),)),
        "block_vals": draw_block_vals(jax.random.fold_in(streams_of[7], 71), 0),
        "block_rows": draw_block_rows(jax.random.fold_in(streams_of[7], 71), 0),
        "block_cols": draw_block_cols(jax.random.fold_in(streams_of[7], 71), 0),
        "block_counts": draw_block_counts(jax.random.fold_in(streams_of[7], 71), 0),
    }


def block_sum(tile_set, block_vals, src_ids, dst_ids, block_counts, transpose):
    feat_dim = tile_set.shape[2]
    slot_ids = jnp.arange(CAP)
    pattern = "kji,kjf->kif" if transpose else "kij,kjf->kif"

    def add_device(running, device_item):
        values, sources, targets, used_slots = device_item
        in_use = (slot_ids[None, :] < used_slots[:, None]).reshape(-1).astype(jnp.float32)
        values = values.reshape(-1, BS, BS).astype(jnp.float32)
        picked = tile_set[sources.reshape(-1)].astype(jnp.float32)
        products = jnp.einsum(pattern, values, picked, precision=lax.Precision.HIGHEST)
        running = running.at[targets.reshape(-1)].add(products * in_use[:, None, None])
        return running, None

    empty_sum = jnp.zeros((NBLOCKS, BS, feat_dim), jnp.float32)
    running, unused = lax.scan(add_device, empty_sum, (block_vals, src_ids, dst_ids, block_counts))
    return running.reshape(NBLOCKS * BS, feat_dim)


def reference(features, weight, grad_out, block_vals, block_rows, block_cols, block_counts):
    feat_tiles = features.reshape(NBLOCKS, BS, F_IN)
    hidden_sum = block_sum(feat_tiles, block_vals, block_cols, block_rows, block_counts, False)
    hidden = hidden_sum.astype(jnp.bfloat16)
    pre_act = jnp.dot(hidden, weight, preferred_element_type=jnp.float32)
    sig_pre = jax.nn.sigmoid(pre_act)
    activations = (pre_act * sig_pre).astype(jnp.bfloat16)
    grad_pre = (grad_out.astype(jnp.float32) * sig_pre * (1.0 + pre_act * (1.0 - sig_pre))).astype(jnp.bfloat16)
    grad_weight = jnp.dot(hidden.T, grad_pre, preferred_element_type=jnp.float32) * (NODES ** -0.5)
    back_rows = jnp.dot(grad_pre, weight.T, preferred_element_type=jnp.float32).astype(jnp.bfloat16)
    back_tiles = back_rows.reshape(NBLOCKS, BS, F_IN)
    grad_sum = block_sum(back_tiles, block_vals, block_rows, block_cols, block_counts, True)
    return activations, grad_sum.astype(jnp.bfloat16), grad_weight
```

```python
import jax
import jax.numpy as jnp
from jax import lax
from jax.experimental import pallas as pl
from jax.experimental.pallas import tpu as pltpu
from jax.sharding import PartitionSpec as P

BF = jnp.bfloat16
F32 = jnp.float32
VMEM = pltpu.VMEM
SMEM = pltpu.SMEM
HBM_MB = 1 << 20
SIDE = 4


def along_z(k):
    return [(t, (t // SIDE) * SIDE + (t % SIDE + k) % SIDE) for t in range(SIDE * SIDE)]


def along_y(k):
    return [(t, ((t // SIDE + k) % SIDE) * SIDE + t % SIDE) for t in range(SIDE * SIDE)]


def along_blk(k):
    count = lax.axis_size("blk")
    return [(b, (b + k) % count) for b in range(count)]


def gather_side(block, route):
    return [block] + [lax.ppermute(block, "team", route(-k)) for k in range(1, SIDE)]


def aggregate_kernel(place, rows, cols, counts, *refs):
    chunks = refs[:12]
    values = refs[12]
    own, *sends = refs[13:17]
    tiles, blocks, total, tile_sems, block_sems = refs[17:]
    order = (1, 0, 2)
    copies = []
    for n, offset in enumerate(order):
        block_copy = pltpu.make_async_copy(
            values.at[offset], blocks.at[offset], block_sems.at[offset]
        )
        block_copy.start()
        group = [block_copy]
        for c in range(SIDE):
            slot = n * SIDE + c
            copy = pltpu.make_async_copy(
                chunks[slot], tiles.at[offset, pl.ds(c * SIDE, SIDE)], tile_sems.at[slot]
            )
            copy.start()
            group.append(copy)
        copies.append(group)
    my_y, my_z = place[0], place[1]
    total[...] = jnp.zeros_like(total)

    def one(offset, k):
        col = cols[offset, k] & 15
        row = rows[offset, k] & 15
        source = (((col >> 2) - my_y) & 3) * SIDE + ((col - my_z) & 3)
        product = jnp.dot(
            blocks[offset, k], tiles[offset, source], preferred_element_type=F32
        )
        total[row] = total[row] + product

    for offset, group in zip(order, copies):
        for copy in group:
            copy.wait()
        if offset == 1:
            for k in range(16):
                one(offset, k)
        else:

            @pl.loop(0, counts[offset])
            def _(k):
                one(offset, k)

    own[...] = total[pl.ds(my_y * SIDE, SIDE)]
    for k in range(1, SIDE):
        sends[k - 1][...] = total[pl.ds(((my_y + k) & 3) * SIDE, SIDE)].astype(BF)


def aggregate(place, chunks, values, rows, cols, counts):
    quarter = chunks[0].shape
    return pl.pallas_call(
        aggregate_kernel,
        in_specs=[pl.BlockSpec(memory_space=SMEM)] * 4
        + [pl.BlockSpec(memory_space=pl.ANY)] * 13,
        out_specs=[pl.BlockSpec(memory_space=VMEM)] * 4,
        out_shape=[jax.ShapeDtypeStruct(quarter, F32)] + [jax.ShapeDtypeStruct(quarter, BF)] * 3,
        scratch_shapes=[
            pltpu.VMEM((3, 16) + quarter[1:], BF),
            pltpu.VMEM(values.shape, BF),
            pltpu.VMEM((16,) + quarter[1:], F32),
            pltpu.SemaphoreType.DMA((12,)),
            pltpu.SemaphoreType.DMA((3,)),
        ],
        compiler_params=pltpu.CompilerParams(vmem_limit_bytes=24 * HBM_MB),
        name="aggregate",
    )(place, rows, cols, counts, *chunks, values)


def fold_kernel(place, own, one, two, three, kept, *sends):
    my_z = place[1]

    def summed(z):
        return (
            own[z]
            + one[z].astype(F32)
            + two[z].astype(F32)
            + three[z].astype(F32)
        )

    kept[...] = summed(my_z)
    for k in range(1, SIDE):
        sends[k - 1][...] = summed((my_z + k) & 3).astype(BF)


def fold(place, own, arrived):
    piece = own.shape[1:]
    return pl.pallas_call(
        fold_kernel,
        in_specs=[pl.BlockSpec(memory_space=SMEM)] + [pl.BlockSpec(memory_space=VMEM)] * 4,
        out_specs=[pl.BlockSpec(memory_space=VMEM)] * 4,
        out_shape=[jax.ShapeDtypeStruct(piece, F32)] + [jax.ShapeDtypeStruct(piece, BF)] * 3,
        compiler_params=pltpu.CompilerParams(vmem_limit_bytes=16 * HBM_MB),
        name="fold",
    )(place, own, *arrived)


def dense_kernel(own, one, two, three, weight, grad_out, act, back, local_grad):
    hidden = (
        own[...] + one[...].astype(F32) + two[...].astype(F32) + three[...].astype(F32)
    ).astype(BF)
    pre_act = jnp.dot(hidden, weight[...], preferred_element_type=F32)
    sig_pre = jax.nn.sigmoid(pre_act)
    act[...] = (pre_act * sig_pre).astype(BF)
    grad_pre = (
        grad_out[...].astype(F32) * sig_pre * (1.0 + pre_act * (1.0 - sig_pre))
    ).astype(BF)
    back[...] = lax.dot_general(
        grad_pre, weight[...], (((1,), (1,)), ((), ())), preferred_element_type=F32
    ).astype(BF)
    local_grad[...] = lax.dot_general(
        hidden, grad_pre, (((0,), (0,)), ((), ())), preferred_element_type=F32
    )


def dense(own, arrived, weight, grad_out):
    piece = own.shape
    return pl.pallas_call(
        dense_kernel,
        in_specs=[pl.BlockSpec(memory_space=VMEM)] * 6,
        out_specs=[pl.BlockSpec(memory_space=VMEM)] * 3,
        out_shape=[
            jax.ShapeDtypeStruct(piece, BF),
            jax.ShapeDtypeStruct(piece, BF),
            jax.ShapeDtypeStruct(weight.shape, F32),
        ],
        compiler_params=pltpu.CompilerParams(vmem_limit_bytes=16 * HBM_MB),
        name="dense",
    )(own, *arrived, weight, grad_out)


def finish_kernel(own, one, two, three, out):
    out[...] = (
        own[...] + one[...].astype(F32) + two[...].astype(F32) + three[...].astype(F32)
    ).astype(BF)


def finish(own, arrived):
    return pl.pallas_call(
        finish_kernel,
        in_specs=[pl.BlockSpec(memory_space=VMEM)] * 4,
        out_specs=pl.BlockSpec(memory_space=VMEM),
        out_shape=jax.ShapeDtypeStruct(own.shape, BF),
        name="finish",
    )(own, *arrived)


def slab_product(piece, place, values, rows, cols, counts):
    rows_dev, width = piece.shape
    quarter = jnp.concatenate(gather_side(piece, along_z), axis=0)
    quarter = quarter.reshape(SIDE, rows_dev, width)
    own_slab = gather_side(quarter, along_y)
    low = [lax.ppermute(c, "blk", along_blk(1)) for c in own_slab]
    high = [lax.ppermute(c, "blk", along_blk(-1)) for c in own_slab]
    own, *sends = aggregate(place, own_slab + low + high, values, rows, cols, counts)
    arrived = [lax.ppermute(s, "team", along_y(k + 1)) for k, s in enumerate(sends)]
    kept, *sends = fold(place, own, arrived)
    return kept, [lax.ppermute(s, "team", along_z(k + 1)) for k, s in enumerate(sends)]


def on_device(features, weight, grad_out, block_vals, block_rows, block_cols, block_counts):
    member = lax.axis_index("team")
    place = jnp.stack([member // SIDE, member % SIDE]).astype(jnp.int32)
    values, rows, cols, counts = block_vals[0], block_rows[0], block_cols[0], block_counts[0]
    kept, arrived = slab_product(features, place, values, rows, cols, counts)
    activations, back_rows, local_grad = dense(kept, arrived, weight, grad_out)
    kept, arrived = slab_product(back_rows, place, values, rows, cols, counts)
    grad_feats = finish(kept, arrived)
    everyone = ("blk", "team")
    devices = lax.axis_size("blk") * lax.axis_size("team")
    nodes = features.shape[0] * devices
    share = weight.shape[0] // devices
    shares = lax.all_to_all(
        local_grad.reshape(devices, share, -1), everyone, 0, 0, tiled=True
    )
    mine = jnp.sum(shares, axis=0, keepdims=True) * nodes ** (-0.5)
    grad_weight = lax.all_to_all(
        jnp.broadcast_to(mine, shares.shape), everyone, 0, 0, tiled=True
    ).reshape(weight.shape)
    return (activations, grad_feats, grad_weight)


def solution(mesh):
    lanes = P(("blk", "team"))
    return jax.shard_map(
        on_device,
        mesh=mesh,
        in_specs=(lanes, P(), lanes, lanes, lanes, lanes, lanes),
        out_specs=(lanes, lanes, P()),
        check_vma=False,
    )
```

```python
import functools

import jax
import jax.numpy as jnp
from jax import lax
from jax.experimental import pallas as pl
from jax.experimental.pallas import tpu as pltpu
from jax.sharding import PartitionSpec as P

BF = jnp.bfloat16
F32 = jnp.float32
VMEM = pltpu.VMEM
SMEM = pltpu.SMEM
MIB = 1 << 20
SIDE = 4
PARTS = 1
TURNS = (1, 3, 2)
SLOTS = 16
COUNTS, ROWS, COLS = 3, 16, 64


def along_z(k):
    return [(t, (t // SIDE) * SIDE + (t % SIDE + k) % SIDE) for t in range(SIDE * SIDE)]


def along_y(k):
    return [(t, ((t // SIDE + k) % SIDE) * SIDE + t % SIDE) for t in range(SIDE * SIDE)]


def flipped(bit):
    return [(b, b ^ bit) for b in range(lax.axis_size("blk"))]


def outer():
    count = lax.axis_size("blk")
    return [(b, (b + 1 if b % 2 else b - 1) % count) for b in range(count)]


def whole(space=VMEM):
    return pl.BlockSpec(memory_space=space)


def call(kernel, outs, operands, specs, scratch=(), limit=16, name=None):
    return pl.pallas_call(
        kernel,
        in_specs=specs,
        out_specs=[whole()] * len(outs),
        out_shape=[jax.ShapeDtypeStruct(shape, kind) for shape, kind in outs],
        scratch_shapes=list(scratch),
        compiler_params=pltpu.CompilerParams(vmem_limit_bytes=limit * MIB),
        name=name or kernel.__name__.removesuffix("_kernel"),
    )(*operands)


def split(value):
    parts = []
    for _ in range(PARTS):
        parts.append(value.astype(BF))
        value = value - parts[-1].astype(F32)
    return jnp.stack(parts)


def joined(parts):
    total = parts[0].astype(F32)
    for n in range(1, PARTS):
        total = total + parts[n].astype(F32)
    return total


def aggregate_kernel(layout, meta, values, *refs):
    chunks = refs[: len(layout)]
    own, *sends = refs[len(layout) : len(layout) + SIDE]
    tiles, blocks, total, tile_sems, block_sem = refs[len(layout) + SIDE :]
    block_copy = pltpu.make_async_copy(values.at[0], blocks, block_sem)
    block_copy.start()
    copies = [[], [], []]
    for chunk, (group, places) in zip(chunks, layout):
        for n, place in enumerate(places):
            copy = pltpu.make_async_copy(
                chunk.at[pl.ds(n * 2 * SIDE, 2 * SIDE)],
                tiles.at[group, pl.ds(place * 2 * SIDE, 2 * SIDE)],
                tile_sems.at[group, place],
            )
            copy.start()
            copies[group].append(copy)
    my_y, my_z, near_offset = meta[0], meta[1], meta[2]
    total[...] = jnp.zeros_like(total)

    def one(group, offset, k):
        at = offset * SLOTS + k
        col = meta[COLS + at] & 15
        row = meta[ROWS + at] & 15
        source = (((col >> 2) - my_y) & 3) * SIDE + ((col - my_z) & 3)
        tile = tiles[group, pl.ds(2 * source, 2)].reshape(total.shape[1:])
        product = jnp.dot(blocks[offset, k], tile, preferred_element_type=F32)
        total[row] = total[row] + product

    block_copy.wait()
    for group in range(3):
        for copy in copies[group]:
            copy.wait()
        if group == 0:
            for k in range(SLOTS):
                one(0, 1, k)
        else:
            offset = near_offset if group == 1 else 2 - near_offset

            @pl.loop(0, meta[COUNTS + offset])
            def _(k):
                one(group, offset, k)

    own[...] = total[pl.ds(my_y * SIDE, SIDE)]
    for k, send in enumerate(sends, 1):
        share = total[pl.ds(((my_y + k) & 3) * SIDE, SIDE)].astype(BF)
        send[...] = share.reshape(send.shape)


def aggregate(meta, slabs, values):
    half, width = slabs[0][0].shape[1:]
    rows_dev = 2 * half
    chunks = [chunk for chunk, _, _ in slabs]
    layout = tuple((group, places) for _, group, places in slabs)
    return call(
        functools.partial(aggregate_kernel, layout),
        [((SIDE, rows_dev, width), F32)] + [((2 * SIDE, half, width), BF)] * 3,
        [meta, values] + chunks,
        [whole(SMEM)] + [whole(pl.ANY)] * (1 + len(chunks)),
        [
            pltpu.VMEM((3, 2 * SLOTS, half, width), BF),
            pltpu.VMEM(values.shape[1:], BF),
            pltpu.VMEM((SLOTS, rows_dev, width), F32),
            pltpu.SemaphoreType.DMA((3, SIDE)),
            pltpu.SemaphoreType.DMA,
        ],
        limit=28,
        name="aggregate",
    )


def fold_body(meta, own, arrived, kept, sends):
    my_z = meta[1]

    def summed(z):
        total = own[z]
        for share in arrived:
            total = total + share[pl.ds(2 * z, 2)].astype(F32).reshape(total.shape)
        return total

    kept[...] = summed(my_z)
    for k, send in enumerate(sends, 1):
        share = summed((my_z + k) & 3).astype(BF)
        send[pl.ds(0, 2)] = share.reshape(2, -1, share.shape[1])


def fold_kernel(meta, own, one, two, three, kept, *sends):
    fold_body(meta, own, (one, two, three), kept, sends)


def fold_grad_kernel(meta, own, one, two, three, grad, kept, kept_grad, *sends):
    fold_body(meta, own, (one, two, three), kept, sends)
    parts = split(grad[...])
    kept_grad[...] = joined(parts)
    for send in sends:
        send[pl.ds(2, PARTS)] = parts


def summed_rows(own, arrived):
    total = own[...]
    for share in arrived:
        total = total + share[pl.ds(0, 2)].astype(F32).reshape(total.shape)
    return total.astype(BF)


def dense_kernel(meta, own, one, two, three, weight, grad_out, act, back, quarter_grad, *rest):
    sends, local_grad = rest[:3], rest[3]
    hidden = summed_rows(own, (one, two, three))
    pre_act = jnp.dot(hidden, weight[...], preferred_element_type=F32)
    sig_pre = jax.nn.sigmoid(pre_act)
    act[...] = (pre_act * sig_pre).astype(BF)
    grad_pre = (
        grad_out[...].astype(F32) * sig_pre * (1.0 + pre_act * (1.0 - sig_pre))
    ).astype(BF)
    rows = lax.dot_general(
        grad_pre, weight[...], (((1,), (1,)), ((), ())), preferred_element_type=F32
    ).astype(BF)
    back[...] = rows
    local_grad[...] = lax.dot_general(
        hidden, grad_pre, (((0,), (0,)), ((), ())), preferred_element_type=F32
    ).reshape(local_grad.shape)
    my_z = meta[1]
    quarter_grad[...] = local_grad[my_z]
    for k, send in enumerate(sends, 1):
        send[pl.ds(0, 2)] = rows.reshape(2, -1, rows.shape[1])
        send[2] = local_grad[(my_z - k) & 3].astype(BF)


def spread_kernel(back, one, two, three, grad, message):
    units = [back[...].reshape(2, -1, back.shape[1])]
    total = grad[...]
    for ref in (one, two, three):
        units.append(ref[pl.ds(0, 2)])
        total = total + ref[2].astype(F32)
    for k, unit in enumerate(units):
        message[pl.ds(2 * k, 2)] = unit
    message[pl.ds(2 * SIDE, PARTS)] = split(total)


def side_of(block, route, order=(1, 2, 3)):
    got = {0: block}
    for k in order:
        got[k] = lax.ppermute(block, "team", route(-k))
    return [got[k] for k in range(SIDE)]


def three_ways(sends, route):
    return [lax.ppermute(s, "team", route(k)) for k, s in enumerate(sends, 1)]


def slabs_of(message):
    near = {0: lax.ppermute(message, "blk", flipped(1))}
    messages = {0: message}
    for k in TURNS:
        messages[k] = lax.ppermute(message, "team", along_y(-k))
    order = (0,) + TURNS
    far = {}
    for k in order:
        far[k] = lax.ppermute(messages[k], "blk", outer())
        if k:
            near[k] = lax.ppermute(messages[k], "blk", flipped(1))
    groups = [(0, messages), (1, near), (2, far)]
    return messages, [(group[k], n, (k,)) for n, group in groups for k in order]


def grad_of(message):
    total = message[2 * SIDE].astype(F32)
    for n in range(1, PARTS):
        total = total + message[2 * SIDE + n].astype(F32)
    return total


def on_device(features, weight, grad_out, block_vals, block_rows, block_cols, block_counts):
    member = lax.axis_index("team")
    near_offset = 2 - 2 * (lax.axis_index("blk") % 2)
    rows_dev, width = features.shape
    devices = lax.axis_size("blk") * lax.axis_size("team")
    meta = jnp.concatenate(
        [
            jnp.stack([member // SIDE, member % SIDE, near_offset]).astype(jnp.int32),
            block_counts.reshape(-1),
            jnp.zeros((ROWS - COUNTS - block_counts.size,), jnp.int32),
            block_rows.reshape(-1),
            block_cols.reshape(-1),
        ]
    )
    small = (rows_dev, width)
    part = weight.shape[0] // SIDE
    half = rows_dev // 2

    quarter = jnp.concatenate(side_of(features, along_z), axis=0)
    quarter = quarter.reshape(2 * SIDE, half, width)
    own, *sends = aggregate(meta, slabs_of(quarter)[1], block_vals)
    arrived = three_ways(sends, along_y)
    kept, *sends = call(
        fold_kernel,
        [(small, F32)] + [((2, half, width), BF)] * 3,
        [meta, own, *arrived],
        [whole(SMEM)] + [whole()] * 4,
    )
    arrived = three_ways(sends, along_z)

    activations, back, quarter_grad, *sends = call(
        dense_kernel,
        [(small, BF), (small, BF), ((part, weight.shape[1]), F32)] + [((3, half, width), BF)] * 3,
        [meta, kept, *arrived, weight, grad_out],
        [whole(SMEM)] + [whole()] * 6,
        [pltpu.VMEM((SIDE, part, weight.shape[1]), F32)],
    )
    arrived = [lax.ppermute(s, "team", along_z(-k)) for k, s in enumerate(sends, 1)]
    [message] = call(
        spread_kernel,
        [((2 * SIDE + PARTS, half, width), BF)],
        [back, *arrived, quarter_grad],
        [whole()] * 5,
    )
    messages, slabs = slabs_of(message)
    zero, one, two, three = [grad_of(messages[k]) for k in range(SIDE)]
    grad = (zero + two) + (one + three)
    for bit in (1, 2):
        grad = grad + lax.ppermute(grad, "blk", flipped(bit))
    meta, grad = lax.optimization_barrier((meta, grad))
    for bit in (8, 4):
        grad = grad + lax.ppermute(grad, "blk", flipped(bit))
    own, *sends = aggregate(meta, slabs, block_vals)
    arrived = three_ways(sends, along_y)
    kept, kept_grad, *sends = call(
        fold_grad_kernel,
        [(small, F32), (grad.shape, F32)] + [((2 + PARTS, half, width), BF)] * 3,
        [meta, own, *arrived, grad],
        [whole(SMEM)] + [whole()] * 5,
    )
    arrived = three_ways(sends, along_z)
    scale = (rows_dev * devices) ** (-0.5)

    def finish_kernel(meta, own, grad, one, two, three, out, grad_weight):
        out[...] = summed_rows(own, (one, two, three))
        my_z = meta[1]
        grad_weight[my_z] = grad[...] * scale
        for k, ref in enumerate((one, two, three), 1):
            grad_weight[(my_z - k) & 3] = joined(ref[pl.ds(2, PARTS)]) * scale

    grad_feats, grad_weight = call(
        finish_kernel,
        [(small, BF), ((SIDE,) + grad.shape, F32)],
        [meta, kept, kept_grad, *arrived],
        [whole(SMEM)] + [whole()] * 5,
    )
    return (activations, grad_feats, grad_weight.reshape(weight.shape))


def solution(mesh):
    lanes = P(("blk", "team"))
    return jax.shard_map(
        on_device,
        mesh=mesh,
        in_specs=(lanes, P(), lanes, lanes, lanes, lanes, lanes),
        out_specs=(lanes, lanes, P()),
        check_vma=False,
    )
```

```python
import functools

import jax
import jax.numpy as jnp
from jax import lax
from jax.experimental import pallas as pl
from jax.experimental.pallas import tpu as pltpu
from jax.sharding import PartitionSpec as P

BF = jnp.bfloat16
F32 = jnp.float32
VMEM = pltpu.VMEM
SMEM = pltpu.SMEM
MIB = 1 << 20
SIDE = 4
PARTS = 1
TURNS = (1, 3, 2)
SLOTS = 16
TOGETHER = 8
COUNTS, ROWS, COLS = 3, 16, 64


def along_z(k):
    return [(t, (t // SIDE) * SIDE + (t % SIDE + k) % SIDE) for t in range(SIDE * SIDE)]


def along_y(k):
    return [(t, ((t // SIDE + k) % SIDE) * SIDE + t % SIDE) for t in range(SIDE * SIDE)]


def flipped(bit):
    return [(b, b ^ bit) for b in range(lax.axis_size("blk"))]


def outer():
    count = lax.axis_size("blk")
    return [(b, (b + 1 if b % 2 else b - 1) % count) for b in range(count)]


def whole(space=VMEM):
    return pl.BlockSpec(memory_space=space)


def call(kernel, outs, operands, specs, scratch=(), limit=16, name=None):
    return pl.pallas_call(
        kernel,
        in_specs=specs,
        out_specs=[whole()] * len(outs),
        out_shape=[jax.ShapeDtypeStruct(shape, kind) for shape, kind in outs],
        scratch_shapes=list(scratch),
        compiler_params=pltpu.CompilerParams(vmem_limit_bytes=limit * MIB),
        name=name or kernel.__name__.removesuffix("_kernel"),
    )(*operands)


def split(value):
    parts = []
    for _ in range(PARTS):
        parts.append(value.astype(BF))
        value = value - parts[-1].astype(F32)
    return jnp.stack(parts)


def joined(parts):
    total = parts[0].astype(F32)
    for n in range(1, PARTS):
        total = total + parts[n].astype(F32)
    return total


def keep_kernel(values, kept, sem):
    copy = pltpu.make_async_copy(values.at[0], kept, sem)
    copy.start()
    copy.wait()


def aggregate_kernel(layout, meta, blocks, *refs):
    chunks = refs[: len(layout)]
    own, *sends = refs[len(layout) : len(layout) + SIDE]
    tiles, total = refs[len(layout) + SIDE :]
    my_y, my_z, near_offset = meta[0], meta[1], meta[2]
    total[...] = jnp.zeros_like(total)

    def one(group, offset, k, count=None):
        at = offset * SLOTS + k
        col = meta[COLS + at] & 15
        row = meta[ROWS + at] & 15
        source = (((col >> 2) - my_y) & 3) * SIDE + ((col - my_z) & 3)
        tile = tiles[group, pl.ds(2 * source, 2)].reshape(total.shape[1:])
        product = jnp.dot(blocks[offset, k], tile, preferred_element_type=F32)
        if count is not None:
            product = jnp.where(k < count, product, 0.0)
        total[row] = total[row] + product

    for group in range(3):
        for chunk, (at, places) in zip(chunks, layout):
            if at == group:
                for n, place in enumerate(places):
                    tiles[group, pl.ds(place * 2 * SIDE, 2 * SIDE)] = chunk[
                        pl.ds(n * 2 * SIDE, 2 * SIDE)
                    ]
        if group == 0:
            for k in range(SLOTS):
                one(0, 1, k)
        else:
            offset = near_offset if group == 1 else 2 - near_offset

            count = meta[COUNTS + offset]

            @pl.loop(0, (count + TOGETHER - 1) // TOGETHER)
            def _(n):
                for k in range(TOGETHER):
                    one(group, offset, n * TOGETHER + k, count)

    own[...] = total[pl.ds(my_y * SIDE, SIDE)]
    for k, send in enumerate(sends, 1):
        share = total[pl.ds(((my_y + k) & 3) * SIDE, SIDE)].astype(BF)
        send[...] = share.reshape(send.shape)


def aggregate(meta, slabs, blocks):
    half, width = slabs[0][0].shape[1:]
    rows_dev = 2 * half
    chunks = [chunk for chunk, _, _ in slabs]
    layout = tuple((group, places) for _, group, places in slabs)
    return call(
        functools.partial(aggregate_kernel, layout),
        [((SIDE, rows_dev, width), F32)] + [((2 * SIDE, half, width), BF)] * 3,
        [meta, blocks] + chunks,
        [whole(SMEM)] + [whole()] * (1 + len(chunks)),
        [
            pltpu.VMEM((3, 2 * SLOTS, half, width), BF),
            pltpu.VMEM((SLOTS, rows_dev, width), F32),
        ],
        limit=28,
        name="aggregate",
    )


def fold_body(meta, own, arrived, kept, sends):
    my_z = meta[1]

    def summed(z):
        total = own[z]
        for share in arrived:
            total = total + share[pl.ds(2 * z, 2)].astype(F32).reshape(total.shape)
        return total

    kept[...] = summed(my_z)
    for k, send in enumerate(sends, 1):
        share = summed((my_z + k) & 3).astype(BF)
        send[pl.ds(0, 2)] = share.reshape(2, -1, share.shape[1])


def fold_kernel(meta, own, one, two, three, kept, *sends):
    fold_body(meta, own, (one, two, three), kept, sends)


def fold_grad_kernel(meta, own, one, two, three, grad, kept, kept_grad, *sends):
    fold_body(meta, own, (one, two, three), kept, sends)
    parts = split(grad[...])
    kept_grad[...] = joined(parts)
    for send in sends:
        send[pl.ds(2, PARTS)] = parts


def summed_rows(own, arrived):
    total = own[...]
    for share in arrived:
        total = total + share[pl.ds(0, 2)].astype(F32).reshape(total.shape)
    return total.astype(BF)


def dense_kernel(meta, own, one, two, three, weight, grad_out, act, back, quarter_grad, *rest):
    sends, local_grad = rest[:3], rest[3]
    hidden = summed_rows(own, (one, two, three))
    pre_act = jnp.dot(hidden, weight[...], preferred_element_type=F32)
    sig_pre = jax.nn.sigmoid(pre_act)
    act[...] = (pre_act * sig_pre).astype(BF)
    grad_pre = (
        grad_out[...].astype(F32) * sig_pre * (1.0 + pre_act * (1.0 - sig_pre))
    ).astype(BF)
    rows = lax.dot_general(
        grad_pre, weight[...], (((1,), (1,)), ((), ())), preferred_element_type=F32
    ).astype(BF)
    back[...] = rows
    local_grad[...] = lax.dot_general(
        hidden, grad_pre, (((0,), (0,)), ((), ())), preferred_element_type=F32
    ).reshape(local_grad.shape)
    my_z = meta[1]
    quarter_grad[...] = local_grad[my_z]
    for k, send in enumerate(sends, 1):
        send[pl.ds(0, 2)] = rows.reshape(2, -1, rows.shape[1])
        send[2] = local_grad[(my_z - k) & 3].astype(BF)


def spread_kernel(back, one, two, three, grad, message):
    units = [back[...].reshape(2, -1, back.shape[1])]
    total = grad[...]
    for ref in (one, two, three):
        units.append(ref[pl.ds(0, 2)])
        total = total + ref[2].astype(F32)
    for k, unit in enumerate(units):
        message[pl.ds(2 * k, 2)] = unit
    message[pl.ds(2 * SIDE, PARTS)] = split(total)


def side_of(block, route, order=(1, 2, 3)):
    got = {0: block}
    for k in order:
        got[k] = lax.ppermute(block, "team", route(-k))
    return [got[k] for k in range(SIDE)]


def three_ways(sends, route):
    return [lax.ppermute(s, "team", route(k)) for k, s in enumerate(sends, 1)]


def slabs_of(message):
    near = {0: lax.ppermute(message, "blk", flipped(1))}
    messages = {0: message}
    for k in TURNS:
        messages[k] = lax.ppermute(message, "team", along_y(-k))
    order = (0,) + TURNS
    far = {}
    for k in order:
        far[k] = lax.ppermute(messages[k], "blk", outer())
        if k:
            near[k] = lax.ppermute(messages[k], "blk", flipped(1))
    groups = [(0, messages), (1, near), (2, far)]
    return messages, [(group[k], n, (k,)) for n, group in groups for k in order]


def grad_of(message):
    total = message[2 * SIDE].astype(F32)
    for n in range(1, PARTS):
        total = total + message[2 * SIDE + n].astype(F32)
    return total


def on_device(features, weight, grad_out, block_vals, block_rows, block_cols, block_counts):
    member = lax.axis_index("team")
    near_offset = 2 - 2 * (lax.axis_index("blk") % 2)
    rows_dev, width = features.shape
    devices = lax.axis_size("blk") * lax.axis_size("team")
    meta = jnp.concatenate(
        [
            jnp.stack([member // SIDE, member % SIDE, near_offset]).astype(jnp.int32),
            block_counts.reshape(-1),
            jnp.zeros((ROWS - COUNTS - block_counts.size,), jnp.int32),
            block_rows.reshape(-1),
            block_cols.reshape(-1),
        ]
    )
    small = (rows_dev, width)
    part = weight.shape[0] // SIDE
    half = rows_dev // 2

    [blocks] = call(
        keep_kernel,
        [(block_vals.shape[1:], BF)],
        [block_vals],
        [whole(pl.ANY)],
        [pltpu.SemaphoreType.DMA],
    )
    quarter = jnp.concatenate(side_of(features, along_z), axis=0)
    quarter = quarter.reshape(2 * SIDE, half, width)
    own, *sends = aggregate(meta, slabs_of(quarter)[1], blocks)
    arrived = three_ways(sends, along_y)
    kept, *sends = call(
        fold_kernel,
        [(small, F32)] + [((2, half, width), BF)] * 3,
        [meta, own, *arrived],
        [whole(SMEM)] + [whole()] * 4,
    )
    arrived = three_ways(sends, along_z)

    activations, back, quarter_grad, *sends = call(
        dense_kernel,
        [(small, BF), (small, BF), ((part, weight.shape[1]), F32)] + [((3, half, width), BF)] * 3,
        [meta, kept, *arrived, weight, grad_out],
        [whole(SMEM)] + [whole()] * 6,
        [pltpu.VMEM((SIDE, part, weight.shape[1]), F32)],
    )
    arrived = [lax.ppermute(s, "team", along_z(-k)) for k, s in enumerate(sends, 1)]
    [message] = call(
        spread_kernel,
        [((2 * SIDE + PARTS, half, width), BF)],
        [back, *arrived, quarter_grad],
        [whole()] * 5,
    )
    messages, slabs = slabs_of(message)
    zero, one, two, three = [grad_of(messages[k]) for k in range(SIDE)]
    grad = (zero + two) + (one + three)
    for bit in (1, 2):
        grad = grad + lax.ppermute(grad, "blk", flipped(bit))
    meta, grad = lax.optimization_barrier((meta, grad))
    for bit in (8, 4):
        grad = grad + lax.ppermute(grad, "blk", flipped(bit))
    own, *sends = aggregate(meta, slabs, blocks)
    arrived = three_ways(sends, along_y)
    kept, kept_grad, *sends = call(
        fold_grad_kernel,
        [(small, F32), (grad.shape, F32)] + [((2 + PARTS, half, width), BF)] * 3,
        [meta, own, *arrived, grad],
        [whole(SMEM)] + [whole()] * 5,
    )
    arrived = three_ways(sends, along_z)
    scale = (rows_dev * devices) ** (-0.5)

    def finish_kernel(meta, own, grad, one, two, three, out, grad_weight):
        out[...] = summed_rows(own, (one, two, three))
        my_z = meta[1]
        grad_weight[my_z] = grad[...] * scale
        for k, ref in enumerate((one, two, three), 1):
            grad_weight[(my_z - k) & 3] = joined(ref[pl.ds(2, PARTS)]) * scale

    grad_feats, grad_weight = call(
        finish_kernel,
        [(small, BF), ((SIDE,) + grad.shape, F32)],
        [meta, kept, kept_grad, *arrived],
        [whole(SMEM)] + [whole()] * 5,
    )
    return (activations, grad_feats, grad_weight.reshape(weight.shape))


def solution(mesh):
    lanes = P(("blk", "team"))
    return jax.shard_map(
        on_device,
        mesh=mesh,
        in_specs=(lanes, P(), lanes, lanes, lanes, lanes, lanes),
        out_specs=(lanes, lanes, P()),
        check_vma=False,
    )
```

```python
import functools

import jax
import jax.numpy as jnp
from jax import lax
from jax.experimental import pallas as pl
from jax.experimental.pallas import tpu as pltpu
from jax.sharding import PartitionSpec as P

BF = jnp.bfloat16
F32 = jnp.float32
VMEM = pltpu.VMEM
SMEM = pltpu.SMEM
MIB = 1 << 20
SIDE = 4
PARTS = 1
TURNS = (3, 1, 2)
SLOTS = 16
TOGETHER = 8
COUNTS, ROWS, COLS = 3, 16, 64


def along_z(k):
    return [(t, (t // SIDE) * SIDE + (t % SIDE + k) % SIDE) for t in range(SIDE * SIDE)]


def along_y(k):
    return [(t, ((t // SIDE + k) % SIDE) * SIDE + t % SIDE) for t in range(SIDE * SIDE)]


def flipped(bit):
    return [(b, b ^ bit) for b in range(lax.axis_size("blk"))]


def outer():
    count = lax.axis_size("blk")
    return [(b, (b + 1 if b % 2 else b - 1) % count) for b in range(count)]


def whole(space=VMEM):
    return pl.BlockSpec(memory_space=space)


def call(kernel, outs, operands, specs, scratch=(), limit=16, name=None):
    return pl.pallas_call(
        kernel,
        in_specs=specs,
        out_specs=[whole()] * len(outs),
        out_shape=[jax.ShapeDtypeStruct(shape, kind) for shape, kind in outs],
        scratch_shapes=list(scratch),
        compiler_params=pltpu.CompilerParams(vmem_limit_bytes=limit * MIB),
        name=name or kernel.__name__.removesuffix("_kernel"),
    )(*operands)


def split(value):
    parts = []
    for _ in range(PARTS):
        parts.append(value.astype(BF))
        value = value - parts[-1].astype(F32)
    return jnp.stack(parts)


def joined(parts):
    total = parts[0].astype(F32)
    for n in range(1, PARTS):
        total = total + parts[n].astype(F32)
    return total


def keep_kernel(values, kept, sem):
    copy = pltpu.make_async_copy(values.at[0], kept, sem)
    copy.start()
    copy.wait()


def aggregate_kernel(layout, meta, blocks, *refs):
    chunks = refs[: len(layout)]
    own, *sends = refs[len(layout) : len(layout) + SIDE]
    tiles, total = refs[len(layout) + SIDE :]
    my_y, my_z, near_offset = meta[0], meta[1], meta[2]
    total[...] = jnp.zeros_like(total)

    def one(group, offset, k, count=None):
        at = offset * SLOTS + k
        col = meta[COLS + at] & 15
        row = meta[ROWS + at] & 15
        source = (((col >> 2) - my_y) & 3) * SIDE + ((col - my_z) & 3)
        tile = tiles[group, pl.ds(2 * source, 2)].reshape(total.shape[1:])
        product = jnp.dot(blocks[offset, k], tile, preferred_element_type=F32)
        if count is not None:
            product = jnp.where(k < count, product, 0.0)
        total[row] = total[row] + product

    for group in range(3):
        for chunk, (at, places) in zip(chunks, layout):
            if at == group:
                for n, place in enumerate(places):
                    tiles[group, pl.ds(place * 2 * SIDE, 2 * SIDE)] = chunk[
                        pl.ds(n * 2 * SIDE, 2 * SIDE)
                    ]
        if group == 0:
            for k in range(SLOTS):
                one(0, 1, k)
        else:
            offset = near_offset if group == 1 else 2 - near_offset

            count = meta[COUNTS + offset]

            @pl.loop(0, (count + TOGETHER - 1) // TOGETHER)
            def _(n):
                for k in range(TOGETHER):
                    one(group, offset, n * TOGETHER + k, count)

    own[...] = total[pl.ds(my_y * SIDE, SIDE)]
    for k, send in enumerate(sends, 1):
        share = total[pl.ds(((my_y + k) & 3) * SIDE, SIDE)].astype(BF)
        send[...] = share.reshape(send.shape)


def aggregate(meta, slabs, blocks):
    half, width = slabs[0][0].shape[1:]
    rows_dev = 2 * half
    chunks = [chunk for chunk, _, _ in slabs]
    layout = tuple((group, places) for _, group, places in slabs)
    return call(
        functools.partial(aggregate_kernel, layout),
        [((SIDE, rows_dev, width), F32)] + [((2 * SIDE, half, width), BF)] * 3,
        [meta, blocks] + chunks,
        [whole(SMEM)] + [whole()] * (1 + len(chunks)),
        [
            pltpu.VMEM((3, 2 * SLOTS, half, width), BF),
            pltpu.VMEM((SLOTS, rows_dev, width), F32),
        ],
        limit=28,
        name="aggregate",
    )


def fold_body(meta, own, arrived, kept, sends):
    my_z = meta[1]

    def summed(z):
        total = own[z]
        for share in arrived:
            total = total + share[pl.ds(2 * z, 2)].astype(F32).reshape(total.shape)
        return total

    kept[...] = summed(my_z)
    for k, send in enumerate(sends, 1):
        share = summed((my_z + k) & 3).astype(BF)
        send[pl.ds(0, 2)] = share.reshape(2, -1, share.shape[1])


def fold_kernel(meta, own, one, two, three, kept, *sends):
    fold_body(meta, own, (one, two, three), kept, sends)


def fold_grad_kernel(meta, own, one, two, three, grad, kept, kept_grad, *sends):
    fold_body(meta, own, (one, two, three), kept, sends)
    parts = split(grad[...])
    kept_grad[...] = joined(parts)
    for send in sends:
        send[pl.ds(2, PARTS)] = parts


def summed_rows(own, arrived):
    total = own[...]
    for share in arrived:
        total = total + share[pl.ds(0, 2)].astype(F32).reshape(total.shape)
    return total.astype(BF)


def dense_kernel(meta, own, one, two, three, weight, grad_out, act, back, quarter_grad, *rest):
    sends, local_grad = rest[:3], rest[3]
    hidden = summed_rows(own, (one, two, three))
    pre_act = jnp.dot(hidden, weight[...], preferred_element_type=F32)
    sig_pre = jax.nn.sigmoid(pre_act)
    act[...] = (pre_act * sig_pre).astype(BF)
    grad_pre = (
        grad_out[...].astype(F32) * sig_pre * (1.0 + pre_act * (1.0 - sig_pre))
    ).astype(BF)
    rows = lax.dot_general(
        grad_pre, weight[...], (((1,), (1,)), ((), ())), preferred_element_type=F32
    ).astype(BF)
    back[...] = rows
    local_grad[...] = lax.dot_general(
        hidden, grad_pre, (((0,), (0,)), ((), ())), preferred_element_type=F32
    ).reshape(local_grad.shape)
    my_z = meta[1]
    quarter_grad[...] = local_grad[my_z]
    for k, send in enumerate(sends, 1):
        send[pl.ds(0, 2)] = rows.reshape(2, -1, rows.shape[1])
        send[2] = local_grad[(my_z - k) & 3].astype(BF)


def spread_kernel(back, one, two, three, grad, message):
    units = [back[...].reshape(2, -1, back.shape[1])]
    total = grad[...]
    for ref in (one, two, three):
        units.append(ref[pl.ds(0, 2)])
        total = total + ref[2].astype(F32)
    for k, unit in enumerate(units):
        message[pl.ds(2 * k, 2)] = unit
    message[pl.ds(2 * SIDE, PARTS)] = split(total)


def join_kernel(zero, one, two, three, quarter):
    for k, ref in enumerate((zero, one, two, three)):
        quarter[pl.ds(2 * k, 2)] = ref[...].reshape(2, -1, ref.shape[1])


def side_of(block, route, order=(1, 2, 3)):
    got = {0: block}
    for k in order:
        got[k] = lax.ppermute(block, "team", route(-k))
    return [got[k] for k in range(SIDE)]


def three_ways(sends, route):
    got = {k: lax.ppermute(sends[k - 1], "team", route(k)) for k in (2, 1, 3)}
    return [got[k] for k in range(1, SIDE)]


def slabs_of(message):
    near = {0: lax.ppermute(message, "blk", flipped(1))}
    messages = {0: message}
    for k in TURNS:
        messages[k] = lax.ppermute(message, "team", along_y(-k))
    order = (0,) + TURNS
    far = {}
    for k in order:
        far[k] = lax.ppermute(messages[k], "blk", outer())
        if k:
            near[k] = lax.ppermute(messages[k], "blk", flipped(1))
    groups = [(0, messages), (1, near), (2, far)]
    return messages, [(group[k], n, (k,)) for n, group in groups for k in order]


def grad_of(message):
    total = message[2 * SIDE].astype(F32)
    for n in range(1, PARTS):
        total = total + message[2 * SIDE + n].astype(F32)
    return total


def on_device(features, weight, grad_out, block_vals, block_rows, block_cols, block_counts):
    member = lax.axis_index("team")
    near_offset = 2 - 2 * (lax.axis_index("blk") % 2)
    rows_dev, width = features.shape
    devices = lax.axis_size("blk") * lax.axis_size("team")
    meta = jnp.concatenate(
        [
            jnp.stack([member // SIDE, member % SIDE, near_offset]).astype(jnp.int32),
            block_counts.reshape(-1),
            jnp.zeros((ROWS - COUNTS - block_counts.size,), jnp.int32),
            block_rows.reshape(-1),
            block_cols.reshape(-1),
        ]
    )
    small = (rows_dev, width)
    part = weight.shape[0] // SIDE
    half = rows_dev // 2

    [blocks] = call(
        keep_kernel,
        [(block_vals.shape[1:], BF)],
        [block_vals],
        [whole(pl.ANY)],
        [pltpu.SemaphoreType.DMA],
    )
    [quarter] = call(
        join_kernel,
        [((2 * SIDE, half, width), BF)],
        side_of(features, along_z),
        [whole()] * SIDE,
    )
    own, *sends = aggregate(meta, slabs_of(quarter)[1], blocks)
    arrived = three_ways(sends, along_y)
    kept, *sends = call(
        fold_kernel,
        [(small, F32)] + [((2, half, width), BF)] * 3,
        [meta, own, *arrived],
        [whole(SMEM)] + [whole()] * 4,
    )
    arrived = three_ways(sends, along_z)

    activations, back, quarter_grad, *sends = call(
        dense_kernel,
        [(small, BF), (small, BF), ((part, weight.shape[1]), F32)] + [((3, half, width), BF)] * 3,
        [meta, kept, *arrived, weight, grad_out],
        [whole(SMEM)] + [whole()] * 6,
        [pltpu.VMEM((SIDE, part, weight.shape[1]), F32)],
    )
    arrived = [lax.ppermute(s, "team", along_z(-k)) for k, s in enumerate(sends, 1)]
    [message] = call(
        spread_kernel,
        [((2 * SIDE + PARTS, half, width), BF)],
        [back, *arrived, quarter_grad],
        [whole()] * 5,
    )
    messages, slabs = slabs_of(message)
    zero, one, two, three = [grad_of(messages[k]) for k in range(SIDE)]
    grad = (zero + two) + (one + three)
    for bit in (1, 2):
        grad = grad + lax.ppermute(grad, "blk", flipped(bit))
    meta, grad = lax.optimization_barrier((meta, grad))
    for bit in (8, 4):
        grad = grad + lax.ppermute(grad, "blk", flipped(bit))
    own, *sends = aggregate(meta, slabs, blocks)
    arrived = three_ways(sends, along_y)
    kept, kept_grad, *sends = call(
        fold_grad_kernel,
        [(small, F32), (grad.shape, F32)] + [((2 + PARTS, half, width), BF)] * 3,
        [meta, own, *arrived, grad],
        [whole(SMEM)] + [whole()] * 5,
    )
    arrived = three_ways(sends, along_z)
    scale = (rows_dev * devices) ** (-0.5)

    def finish_kernel(meta, own, grad, one, two, three, out, grad_weight):
        out[...] = summed_rows(own, (one, two, three))
        my_z = meta[1]
        grad_weight[my_z] = grad[...] * scale
        for k, ref in enumerate((one, two, three), 1):
            grad_weight[(my_z - k) & 3] = joined(ref[pl.ds(2, PARTS)]) * scale

    grad_feats, grad_weight = call(
        finish_kernel,
        [(small, BF), ((SIDE,) + grad.shape, F32)],
        [meta, kept, kept_grad, *arrived],
        [whole(SMEM)] + [whole()] * 5,
    )
    return (activations, grad_feats, grad_weight.reshape(weight.shape))


def solution(mesh):
    lanes = P(("blk", "team"))
    return jax.shard_map(
        on_device,
        mesh=mesh,
        in_specs=(lanes, P(), lanes, lanes, lanes, lanes, lanes),
        out_specs=(lanes, lanes, P()),
        check_vma=False,
    )
```
